32 devices in a mesh: row: 4 (over y, core), col: 8 (over z, x).
Axes of the slice: x: 2, y: 2, z: 4, core: 2. Of those that a mesh axis runs over, the one named last changes fastest.
Arguments:
- occ_coeffs: bfloat16 [49152, 20480], P('row', 'col'), may hold values from -0.21875 to 0.21875
- colloc: bfloat16 [256, 1024, 512], P(('row', 'col')), may hold values from -6 to 6
- grid_points: float32 [256, 3, 512], P(('row', 'col')), may hold values from -4 to 4
- grid_weights: float32 [256, 512], P(('row', 'col')), may hold values from 0.01 to 0.1
- charge_sites: float32 [3, 512], replicated, may hold values from -4 to 4
- charge_proj: bfloat16 [512, 128], replicated, may hold values from -0.5 to 0.5
- shell_lists: int32 [256, 16], P(('row', 'col')), may hold values from 0 to 767, as said below
- point_counts: int32 [256], P(('row', 'col')), may hold values from 1 to 512, as said below
Outputs:
- exchange_slab: float32 [49152, 128], P(('row', 'col'))
The draws below stay inside these ranges and needn't reach their ends.
Inputs may be any that keep to these rules, and one draw needn't show every extreme that they name: `shell_lists`: batches b * 8 to b * 8 + 7 belong to the b-th device in row+col order, and the blocks named by one device's batches are all different. Owner device o holds blocks o * 24 to o * 24 + 23; one device's batches name at most 8 blocks of one owner, and in every draw one owner gets exactly 8 from every device. `point_counts`: points of a batch beyond its count are not part of it.
All inputs are finite; a program needn't handle non-finite values.
Results may differ from the reference program's by a relative error of at most 0.0045.
Values may be sent and summed in bfloat16 or wider, within the bound.
A program may use at most 128 MiB of HBM per device.

```python
import math
import jax
import jax.numpy as jnp
from jax import lax

NBF = 49152
NOCC = 20480
SH = 64
NSIG = 16
SLAB = 128
BATCH_DEV = 8
PTS = 512
NAUX = 512
BATCHES = 256
OWN_BLOCKS = 24
CAP = 8
N_ROW = 4
N_COL = 8


def draw_shell_lists(key, part):
    owners = N_ROW * N_COL
    half = CAP // 2
    common_owner = jax.random.randint(jax.random.fold_in(key, 7), (), 0, owners)

    def one_device(device):
        device_key = jax.random.fold_in(jax.random.fold_in(key, 11), device)
        key_order, key_shift, key_offset, key_place = jax.random.split(device_key, 4)
        order = jax.random.permutation(key_order, owners)
        order = (order - order[0] + common_owner) % owners
        shifts = jax.random.randint(key_shift, (owners // 2,), -half, half + 1)
        shifts = shifts.at[0].set(half)
        counts = jnp.zeros((owners,), jnp.int32)
        counts = counts.at[order[0::2]].set(half + shifts)
        counts = counts.at[order[1::2]].set(half - shifts)
        offsets = jax.random.randint(key_offset, (owners,), 0, OWN_BLOCKS)
        places = jnp.arange(CAP)
        table = jnp.arange(owners)[:, None] * OWN_BLOCKS + (places[None, :] + offsets[:, None]) % OWN_BLOCKS
        valid = places[None, :] < counts[:, None]
        ranking = jnp.argsort(jnp.where(valid, 0, 1).reshape(-1), stable=True)
        picked = table.reshape(-1)[ranking[:BATCH_DEV * NSIG]]
        picked = jax.random.permutation(key_place, picked)
        return jnp.sort(picked.reshape(BATCH_DEV, NSIG), axis=1)
    lists = jax.vmap(one_device)(jnp.arange(owners))
    return lists.reshape(BATCHES, NSIG).astype(jnp.int32)


def draw_point_counts(key, part):
    owners = N_ROW * N_COL
    key_level, key_raw, key_pick = jax.random.split(jax.random.fold_in(key, 23), 3)
    levels = jax.random.randint(key_level, (owners, 1), 1, 5)
    tops = jnp.maximum(levels * PTS // 4, 1)
    raw = jax.random.randint(key_raw, (owners, BATCH_DEV), 0, PTS)
    counts = (1 + raw % tops).reshape(-1)
    chosen = jax.random.randint(key_pick, (), 0, BATCHES)
    counts = counts.at[chosen].set(PTS)
    return counts.astype(jnp.int32)


def steps_of(stream_key, extent, shards, smallest, high):
    def one(dim, blocks):
        draws = jax.random.uniform(jax.random.fold_in(jax.random.fold_in(stream_key, 6), dim), (blocks,), jnp.float32, smallest / len(shards), high / len(shards))
        return jnp.repeat(jnp.exp(draws), extent[dim] // blocks).reshape((-1,) + (1,) * (len(extent) - dim - 1))

    factor_of = one(*shards[0])
    for cut in shards[1:]:
        factor_of = factor_of * one(*cut)
    return factor_of


def noise(stream_key, extent, spread, limit, cuts=(), held_as=jnp.bfloat16):
    array = jax.random.normal(stream_key, extent, jnp.float32) * spread
    if len(cuts) > 0:
        array = steps_of(stream_key, extent, cuts, -0.22, 0.18) * array
    return jnp.clip(array, min=-limit, max=limit).astype(held_as)


def setup_inputs(seed: int = 0) -> dict:
    keys = jax.random.split(jax.random.key(seed), 9)
    occ_coeffs = noise(keys[0], (NBF, NOCC), ((NOCC * NSIG * SH) ** -0.25), 0.21875, ((0, 4), (1, 8)))
    colloc = noise(keys[1], (BATCHES, NSIG * SH, PTS), 1.0, 6.0, ((0, 32),))
    grid_points = jnp.clip(jax.random.uniform(keys[2], (BATCHES, 3, PTS), jnp.float32, -4.0, 4.0) * steps_of(keys[2], (BATCHES, 3, PTS), ((0, 32),), -0.4, 0.0), -4.0, 4.0)
    grid_weights = jnp.clip(jnp.exp(math.log(0.1) - 2.3025851 * jax.random.uniform(keys[3], (BATCHES, PTS), jnp.float32) ** steps_of(keys[3], (BATCHES, PTS), ((0, 32),), -0.2, 0.2)), 0.01, 0.1)
    charge_sites = jnp.clip(jax.random.uniform(keys[4], (3, NAUX), jnp.float32, -4.0, 4.0), -4.0, 4.0)
    charge_proj = noise(keys[5], (NAUX, SLAB), SLAB ** -0.5, 0.5)
    shell_lists = draw_shell_lists(jax.random.fold_in(keys[8], 71), 0)
    point_counts = draw_point_counts(jax.random.fold_in(keys[8], 71), 0)
    return dict(occ_coeffs=occ_coeffs, colloc=colloc, grid_points=grid_points, grid_weights=grid_weights, charge_sites=charge_sites, charge_proj=charge_proj, shell_lists=shell_lists, point_counts=point_counts)


smear_sq = 0.25

def potential(points, charge_sites):
    dist_sq = (points[0][None, :] - charge_sites[0][:, None]) ** 2
    dist_sq = dist_sq + (points[1][None, :] - charge_sites[1][:, None]) ** 2
    dist_sq = dist_sq + (points[2][None, :] - charge_sites[2][:, None]) ** 2
    return lax.rsqrt(dist_sq + smear_sq)

def reference(occ_coeffs, colloc, grid_points, grid_weights, charge_sites, charge_proj, shell_lists, point_counts):
    density = jnp.dot(occ_coeffs, occ_coeffs[:SLAB].T, preferred_element_type=jnp.float32).astype(jnp.bfloat16)
    blocks = density.reshape(NBF // SH, SH, SLAB)

    def one_batch(carry, item):
        block_ids, batch_colloc, batch_points, batch_weights, count = item
        fetched = blocks[block_ids].reshape(NSIG * SH, SLAB)
        field = lax.dot_general(fetched, batch_colloc, (((0,), (0,)), ((), ())), preferred_element_type=jnp.float32).astype(jnp.bfloat16)
        projected = jnp.dot(charge_proj, field, preferred_element_type=jnp.float32)
        live = (jnp.arange(PTS) < count).astype(jnp.float32)
        charges = (projected * potential(batch_points, charge_sites) * (batch_weights * live)[None, :]).astype(jnp.bfloat16)
        spread_back = lax.dot_general(charge_proj, charges, (((0,), (0,)), ((), ())), preferred_element_type=jnp.float32).astype(jnp.bfloat16)
        term = lax.dot_general(batch_colloc, spread_back, (((1,), (1,)), ((), ())), preferred_element_type=jnp.float32)
        carry = carry.at[block_ids].add(term.reshape(NSIG, SH * SLAB))
        return (carry, None)
    start_value = jnp.zeros((NBF // SH, SH * SLAB), jnp.float32)
    summed, _ = lax.scan(one_batch, start_value, (shell_lists, colloc, grid_points, grid_weights, point_counts))
    return summed.reshape(NBF, SLAB)
```

```python
import functools

import jax
import jax.numpy as jnp
from jax import lax
from jax.experimental import pallas as pl
from jax.experimental.pallas import tpu as pltpu
from jax.sharding import PartitionSpec as P

SH = 64
NSIG = 16
SMEAR_SQ = 0.25
MESH = pl.DeviceIdType.MESH
F32 = jnp.float32
BF16 = jnp.bfloat16
VMEM_BYTES = 58 * 1024 * 1024


class Place:
    def __init__(self, rows, cols):
        self.n = rows // 2
        self.A = cols // self.n
        self.cols = cols
        row, col = lax.axis_index("row"), lax.axis_index("col")
        self.y, self.core = row // 2, row % 2
        self.a, self.b = col // self.n, col % self.n

    def device(self, y, core, a, b):
        return (y * 2 + core, a * self.n + b)

    def mine(self):
        return self.y, self.core, self.a, self.b

    def sides(self, core):
        return self.y * (1 - core) + self.b * core, self.b * (1 - core) + self.y * core

    def from_sides(self, core, outer, inner):
        return outer * (1 - core) + inner * core, inner * (1 - core) + outer * core

    def owner(self, y, core, a, b):
        return (y * 2 + core) * self.cols + a * self.n + b

    def greet(self):
        y, c, a, b = self.mine()
        peers = [(y, 1 - c, a, b)]
        peers += [(y, c, (a + d) % self.A, b) for d in range(1, self.A)]
        peers += [(y, c, a, (b + d) % self.n) for d in range(1, self.n)]
        peers += [((y + d) % self.n, c, a, b) for d in range(1, self.n)]
        peers += [((y + d) % self.n, 1 - c, a, b) for d in range(1, self.n)]
        barrier = pltpu.get_barrier_semaphore()
        for peer in peers:
            pl.semaphore_signal(barrier, inc=1, device_id=self.device(*peer), device_id_type=MESH)
        pl.semaphore_wait(barrier, len(peers))


def others_first(n):
    return [*range(1, n), 0]


def remote(src, dst, send_sem, recv_sem, device):
    return pltpu.make_async_remote_copy(
        src_ref=src, dst_ref=dst, send_sem=send_sem, recv_sem=recv_sem, device_id=device, device_id_type=MESH
    )


def density_kernel(
    rows, cols, occ, full, held, win, xsend, xrecv, acc, zsend, zrecv, shard,
    load_sem, wsend, wrecv, xs_sem, xr_sem, zs_sem, zr_sem, gs_sem, gr_sem, own_sem,
):
    at = Place(rows, cols)
    n, A = at.n, at.A
    y, core, a, b = at.mine()
    own_rows, slab = shard.shape
    half = slab // 2
    depth = held.shape[0]
    sibling = at.device(y, 1 - core, a, b)
    blocks = [(db, dz) for db in others_first(n) for dz in others_first(A)]

    def load(k):
        db, dz = blocks[k]
        col = (a + dz) % A * n + (b + db) % n
        start = pl.multiple_of(col * own_rows, own_rows)
        return pltpu.make_async_copy(occ.at[pl.ds(start, own_rows)], held.at[k % depth], load_sem.at[k % depth])

    for k in range(min(depth, len(blocks))):
        load(k).start()
    at.greet()

    def part(ref, h):
        return ref.at[pl.ds(h * half, half)]

    root = (y == 0) & (core == 0)
    beside = (y == 0) & (core == 1)

    def window_sends():
        sends = []
        for d in range(1, n):
            for h in range(2):
                sends.append((h, at.device((y + d) % n, h, a, b)))
        sends += [(0, sibling), (1, sibling)]
        return [
            remote(part(occ, h), part(win, h), wsend.at[i], wrecv.at[h], device)
            for i, (h, device) in enumerate(sends)
        ]

    def window_wait(h):
        remote(part(occ, h), part(win, h), wsend.at[0], wrecv.at[h], sibling).wait_recv()

    def window_forward(h):
        return remote(part(win, h), part(win, h), wsend.at[0], wrecv.at[h], sibling)

    @pl.when(root)
    def _():
        for send in window_sends():
            send.start()
        keep = pltpu.make_async_copy(occ.at[pl.ds(0, slab)], win, own_sem.at[0])
        keep.start()
        keep.wait()

    @pl.when(beside)
    def _():
        window_wait(0)
        window_wait(1)

    for h in range(2):
        @pl.when((y > 0) & (core == h))
        def _(h=h):
            window_wait(h)
            window_forward(h).start()
            window_wait(1 - h)

    tile = 512 if own_rows % 512 == 0 else own_rows

    def x_copy(db, dz):
        slot = (db - 1) * A + (a + dz) % A
        device = at.device(y, core, a, (b + db) % n)
        return remote(xsend.at[slot], xrecv.at[slot], xs_sem.at[slot], xr_sem.at[slot], device)

    for k, (db, dz) in enumerate(blocks):
        load(k).wait()
        slot = (db - 1) * A + (a + dz) % A

        @pl.loop(0, own_rows // tile)
        def _(t, k=k, db=db, dz=dz, slot=slot):
            window_rows = pl.ds(pl.multiple_of(t * tile, tile), tile)
            value = lax.dot_general(
                held[k % depth, window_rows, :], win[...], (((1,), (1,)), ((), ())), preferred_element_type=F32
            )
            if db:
                xsend[slot, window_rows, :] = value.astype(BF16)
            else:
                acc[dz, window_rows, :] = value

        if k + depth < len(blocks):
            load(k + depth).start()
        if db:
            x_copy(db, dz).start()

    def z_copy(dz):
        device = at.device(y, core, (a + dz) % A, b)
        return remote(zsend.at[dz - 1], zrecv.at[dz - 1], zs_sem.at[dz - 1], zr_sem.at[dz - 1], device)

    for dz in others_first(A):
        for db in range(1, n):
            x_copy(db, dz).wait_recv()
        total = acc[dz]
        for db in range(1, n):
            total = total + xrecv[(db - 1) * A + (a + dz) % A].astype(F32)
        if dz:
            zsend[dz - 1] = total.astype(BF16)
            z_copy(dz).start()
        else:
            acc[0] = total
    total = acc[0]
    for dz in range(1, A):
        z_copy(dz).wait_recv()
        total = total + zrecv[dz - 1].astype(F32)
    shard[...] = total.astype(BF16)

    outer, inner = at.sides(core)
    counter = [0]
    pending = []

    def rows_of(owner):
        return full.at[pl.ds(pl.multiple_of(owner * own_rows, own_rows), own_rows)]

    def forward(src, owner, device):
        i = counter[0]
        counter[0] += 1
        copy = remote(src, rows_of(owner), gs_sem.at[i], gr_sem.at[owner], device)
        copy.start()
        pending.append(copy)

    def arrived(owner):
        remote(rows_of(owner), rows_of(owner), gs_sem.at[0], gr_sem.at[owner], sibling).wait_recv()

    def owner_at(do, di, dz):
        py, pb = at.from_sides(core, (outer + do) % n, (inner + di) % n)
        return at.owner(py, core, (a + dz) % A, pb)

    def device_at(do, di, dz):
        py, pb = at.from_sides(core, (outer + do) % n, (inner + di) % n)
        return at.device(py, core, (a + dz) % A, pb)

    mine = at.owner(y, core, a, b)
    keep = pltpu.make_async_copy(shard, rows_of(mine), own_sem.at[0])
    keep.start()
    for do in range(n):
        for di in range(n):
            for dz in range(A):
                owner = owner_at(-do, -di, -dz)
                if do or di or dz:
                    arrived(owner)
                    src = rows_of(owner)
                else:
                    src = shard
                    for d in range(1, A):
                        forward(src, owner, device_at(0, 0, d))
                if not do and not di:
                    for d in range(1, n):
                        forward(src, owner, device_at(0, d, 0))
                if not do:
                    for d in range(1, n):
                        forward(src, owner, device_at(d, 0, 0))
                forward(src, owner, sibling)
    for py in range(n):
        for pb in range(n):
            for pa in range(A):
                arrived(at.owner(py, 1 - core, pa, pb))

    keep.wait()
    for copy in pending:
        copy.wait_send()
    for db, dz in blocks:
        if db:
            x_copy(db, dz).wait_send()
    for dz in range(1, A):
        z_copy(dz).wait_send()

    @pl.when(root)
    def _():
        for send in window_sends():
            send.wait_send()

    for h in range(2):
        @pl.when((y > 0) & (core == h))
        def _(h=h):
            window_forward(h).wait_send()


def gathered_density(occ_coeffs, slab):
    rows, cols = lax.axis_size("row"), lax.axis_size("col")
    n = rows // 2
    A = cols // n
    group_rows, depth = occ_coeffs.shape
    own_rows = group_rows // cols
    owners = rows * cols
    sends = A - 1 + A * (n - 1) + A * n * (n - 1) + A * n * n
    dma = pltpu.SemaphoreType.DMA
    return pl.pallas_call(
        functools.partial(density_kernel, rows, cols),
        out_shape=jax.ShapeDtypeStruct((group_rows * rows, slab), BF16),
        in_specs=[pl.BlockSpec(memory_space=pl.ANY)],
        out_specs=pl.BlockSpec(memory_space=pl.ANY),
        scratch_shapes=[
            pltpu.VMEM((4, own_rows, depth), BF16),
            pltpu.VMEM((slab, depth), BF16),
            pltpu.VMEM(((n - 1) * A, own_rows, slab), BF16),
            pltpu.VMEM(((n - 1) * A, own_rows, slab), BF16),
            pltpu.VMEM((A, own_rows, slab), F32),
            pltpu.VMEM((A - 1, own_rows, slab), BF16),
            pltpu.VMEM((A - 1, own_rows, slab), BF16),
            pltpu.VMEM((own_rows, slab), BF16),
            dma((4,)),
            dma((2 * n,)),
            dma((2,)),
            dma(((n - 1) * A,)),
            dma(((n - 1) * A,)),
            dma((A - 1,)),
            dma((A - 1,)),
            dma((sends,)),
            dma((owners,)),
            dma((1,)),
        ],
        compiler_params=pltpu.CompilerParams(
            collective_id=0, has_side_effects=True, vmem_limit_bytes=VMEM_BYTES
        ),
        name="density_everywhere",
    )(occ_coeffs)


def batch_kernel(
    lists, counts, full, colloc, points, weights, sites, proj, dense, fetched, term, fetch_sem
):
    i = pl.program_id(0)
    steps = pl.num_programs(0)
    total_points = colloc.shape[2]
    chunk = min(256, total_points)

    def fetch(step, s):
        start = pl.multiple_of(lists[step * NSIG + s] * SH, SH)
        return pltpu.make_async_copy(
            full.at[pl.ds(start, SH)], fetched.at[step % 2, pl.ds(s * SH, SH)], fetch_sem.at[step % 2, s]
        )

    @pl.when(i == 0)
    def _():
        for s in range(NSIG):
            fetch(i, s).start()
        blank = dense.shape[0] // 64

        @pl.loop(0, 64)
        def _(t):
            dense[pl.ds(pl.multiple_of(t * blank, blank), blank), :] = jnp.zeros((blank, dense.shape[1]), dense.dtype)

    @pl.when(i + 1 < steps)
    def _():
        for s in range(NSIG):
            fetch(i + 1, s).start()

    for s in range(NSIG):
        fetch(i, s).wait()
    count = counts[i]

    def point_chunk(j):
        cut = slice(j * chunk, (j + 1) * chunk)
        values = colloc[0, :, cut]
        field = lax.dot_general(
            fetched[i % 2], values, (((0,), (0,)), ((), ())), preferred_element_type=F32
        ).astype(BF16)
        projected = jnp.dot(proj[...], field, preferred_element_type=F32)
        live = (j * chunk + lax.broadcasted_iota(jnp.int32, (1, chunk), 1) < count).astype(F32)
        dist_sq = (points[0, 0:1, cut] - sites[:, 0:1]) ** 2
        dist_sq = dist_sq + (points[0, 1:2, cut] - sites[:, 1:2]) ** 2
        dist_sq = dist_sq + (points[0, 2:3, cut] - sites[:, 2:3]) ** 2
        kernel = lax.rsqrt(dist_sq + SMEAR_SQ)
        charges = (projected * kernel * (weights[0, :, cut] * live)).astype(BF16)
        spread = lax.dot_general(
            proj[...], charges, (((0,), (0,)), ((), ())), preferred_element_type=F32
        ).astype(BF16)
        return lax.dot_general(values, spread, (((1,), (1,)), ((), ())), preferred_element_type=F32)

    term[...] = point_chunk(0)
    for j in range(1, total_points // chunk):
        @pl.when(count > j * chunk)
        def _(j=j):
            term[...] += point_chunk(j)

    for s in range(NSIG):
        start = pl.multiple_of(lists[i * NSIG + s] * SH, SH)
        dense[pl.ds(start, SH), :] = term[s * SH:(s + 1) * SH, :].astype(dense.dtype)


def batch_terms(full, colloc, grid_points, grid_weights, charge_sites, charge_proj, shell_lists, point_counts):
    batches, func_rows, total_points = colloc.shape
    slab = full.shape[1]
    aux = charge_proj.shape[0]
    return pl.pallas_call(
        batch_kernel,
        out_shape=jax.ShapeDtypeStruct(full.shape, BF16),
        grid_spec=pltpu.PrefetchScalarGridSpec(
            num_scalar_prefetch=2,
            grid=(batches,),
            in_specs=[
                pl.BlockSpec(memory_space=pl.ANY),
                pl.BlockSpec((1, func_rows, total_points), lambda i, *_: (i, 0, 0)),
                pl.BlockSpec((1, 3, total_points), lambda i, *_: (i, 0, 0)),
                pl.BlockSpec((1, 1, total_points), lambda i, *_: (i, 0, 0)),
                pl.BlockSpec((aux, 3), lambda i, *_: (0, 0)),
                pl.BlockSpec((aux, slab), lambda i, *_: (0, 0)),
            ],
            out_specs=pl.BlockSpec(full.shape, lambda i, *_: (0, 0)),
            scratch_shapes=[
                pltpu.VMEM((2, func_rows, slab), BF16),
                pltpu.VMEM((func_rows, slab), F32),
                pltpu.SemaphoreType.DMA((2, NSIG)),
            ],
        ),
        compiler_params=pltpu.CompilerParams(vmem_limit_bytes=VMEM_BYTES),
        name="batch_terms",
    )(
        shell_lists.reshape(-1), point_counts, full, colloc, grid_points,
        grid_weights[:, None, :], charge_sites.T, charge_proj,
    )


def reduce_kernel(
    rows, cols, dense, out, own, r0, s1, r1, s2, r2, s3, r3,
    own_sem, s0_sem, r0_sem, s1_sem, r1_sem, s2_sem, r2_sem, s3_sem, r3_sem,
):
    at = Place(rows, cols)
    n, A = at.n, at.A
    y, core, a, b = at.mine()
    own_rows = out.shape[0]
    outer, inner = at.sides(core)
    sibling = at.device(y, 1 - core, a, b)
    order = [(do, di, dz) for do in others_first(n) for di in others_first(n) for dz in others_first(A)]

    def shard_of(side, do, di, dz):
        so, si = at.sides(side)
        py, pb = at.from_sides(side, (so + do) % n, (si + di) % n)
        pa = (a + dz) % A
        return at.owner(py, side, pa, pb), (py * A + pa) * n + pb

    def rows_of(owner):
        return dense.at[pl.ds(pl.multiple_of(owner * own_rows, own_rows), own_rows)]

    def own_load(k):
        owner, slot = shard_of(core, *order[k])
        return pltpu.make_async_copy(rows_of(owner), own.at[slot], own_sem.at[slot])

    def pair_copy(k):
        owner, slot = shard_of(1 - core, *order[k])
        return remote(rows_of(owner), r0.at[slot], s0_sem.at[slot], r0_sem.at[slot], sibling)

    def pair_wait(slot):
        remote(r0.at[slot], r0.at[slot], s0_sem.at[slot], r0_sem.at[slot], sibling).wait_recv()

    def peer(do, di, dz):
        py, pb = at.from_sides(core, (outer + do) % n, (inner + di) % n)
        return at.device(py, core, (a + dz) % A, pb)

    def outer_copy(do, di, dz):
        slot = ((do - 1) * n + (inner + di) % n) * A + (a + dz) % A
        return remote(s1.at[slot], r1.at[slot], s1_sem.at[slot], r1_sem.at[slot], peer(do, 0, 0))

    def inner_copy(di, dz):
        slot = (di - 1) * A + (a + dz) % A
        return remote(s2.at[slot], r2.at[slot], s2_sem.at[slot], r2_sem.at[slot], peer(0, di, 0))

    def last_copy(dz):
        return remote(s3.at[dz - 1], r3.at[dz - 1], s3_sem.at[dz - 1], r3_sem.at[dz - 1], peer(0, 0, dz))

    for k in range(len(order)):
        own_load(k).start()
    at.greet()
    for k in range(len(order)):
        pair_copy(k).start()

    def outer_slot(d, di, dz):
        return ((d - 1) * n + (inner + di) % n) * A + (a + dz) % A

    def inner_slot(d, dz):
        return (d - 1) * A + (a + dz) % A

    for k, (do, di, dz) in enumerate(order):
        _, slot = shard_of(core, do, di, dz)
        own_load(k).wait()
        pair_wait(slot)
        total = own[slot].astype(F32) + r0[slot].astype(F32)
        if do:
            s1[outer_slot(do, di, dz)] = total.astype(BF16)
            outer_copy(do, di, dz).start()
            continue
        for d in range(1, n):
            outer_copy(d, di, dz).wait_recv()
            total = total + r1[outer_slot(d, di, dz)].astype(F32)
        if di:
            s2[inner_slot(di, dz)] = total.astype(BF16)
            inner_copy(di, dz).start()
            continue
        for d in range(1, n):
            inner_copy(d, dz).wait_recv()
            total = total + r2[inner_slot(d, dz)].astype(F32)
        if dz:
            s3[dz - 1] = total.astype(BF16)
            last_copy(dz).start()
            continue
        for d in range(1, A):
            last_copy(d).wait_recv()
            total = total + r3[d - 1].astype(F32)
        out[...] = total

    for k, (do, di, dz) in enumerate(order):
        pair_copy(k).wait_send()
        if do:
            outer_copy(do, di, dz).wait_send()
        elif di:
            inner_copy(di, dz).wait_send()
        elif dz:
            last_copy(dz).wait_send()


def reduced_to_owners(dense):
    rows, cols = lax.axis_size("row"), lax.axis_size("col")
    n = rows // 2
    A = cols // n
    slab = dense.shape[1]
    own_rows = dense.shape[0] // (rows * cols)
    half = rows * cols // 2
    dma = pltpu.SemaphoreType.DMA

    def buffer(count):
        return pltpu.VMEM((count, own_rows, slab), BF16)

    outer, inner = (n - 1) * n * A, (n - 1) * A
    return pl.pallas_call(
        functools.partial(reduce_kernel, rows, cols),
        out_shape=jax.ShapeDtypeStruct((own_rows, slab), F32),
        in_specs=[pl.BlockSpec(memory_space=pl.ANY)],
        out_specs=pl.BlockSpec(memory_space=pltpu.VMEM),
        scratch_shapes=[
            buffer(half), buffer(half),
            buffer(outer), buffer(outer),
            buffer(inner), buffer(inner),
            buffer(A - 1), buffer(A - 1),
            dma((half,)), dma((half,)), dma((half,)),
            dma((outer,)), dma((outer,)),
            dma((inner,)), dma((inner,)),
            dma((A - 1,)), dma((A - 1,)),
        ],
        compiler_params=pltpu.CompilerParams(
            collective_id=1, has_side_effects=True, vmem_limit_bytes=VMEM_BYTES
        ),
        name="reduce_to_owners",
    )(dense)


def on_device(
    occ_coeffs, colloc, grid_points, grid_weights, charge_sites, charge_proj, shell_lists, point_counts
):
    full = gathered_density(occ_coeffs, charge_proj.shape[1])
    dense = batch_terms(
        full, colloc, grid_points, grid_weights, charge_sites, charge_proj, shell_lists, point_counts
    )
    return reduced_to_owners(dense)


def solution(mesh):
    placed = (
        P("row", "col"),
        P(("row", "col"), None, None),
        P(("row", "col"), None, None),
        P(("row", "col"), None),
        P(),
        P(),
        P(("row", "col"), None),
        P(("row", "col")),
    )
    return jax.shard_map(
        on_device, mesh=mesh, in_specs=placed, out_specs=P(("row", "col"), None), check_vma=False
    )
```

```python
import functools

import jax
import jax.numpy as jnp
from jax import lax
from jax.experimental import pallas as pl
from jax.experimental.pallas import tpu as pltpu
from jax.sharding import PartitionSpec as P

SH = 64
NSIG = 16
SMEAR_SQ = 0.25
MESH = pl.DeviceIdType.MESH
F32 = jnp.float32
BF16 = jnp.bfloat16
VMEM_BYTES = 58 * 1024 * 1024
HELD = 12


class Place:
    def __init__(self, rows, cols):
        self.n = rows // 2
        self.A = cols // self.n
        self.cols = cols
        row, col = lax.axis_index("row"), lax.axis_index("col")
        self.y, self.core = row // 2, row % 2
        self.a, self.b = col // self.n, col % self.n

    def device(self, y, core, a, b):
        return (y * 2 + core, a * self.n + b)

    def mine(self):
        return self.y, self.core, self.a, self.b

    def sides(self, core):
        return self.y * (1 - core) + self.b * core, self.b * (1 - core) + self.y * core

    def from_sides(self, core, outer, inner):
        return outer * (1 - core) + inner * core, inner * (1 - core) + outer * core

    def owner(self, y, core, a, b):
        return (y * 2 + core) * self.cols + a * self.n + b

    def greet(self):
        y, c, a, b = self.mine()
        peers = [(y, 1 - c, a, b)]
        peers += [(y, c, (a + d) % self.A, b) for d in range(1, self.A)]
        peers += [(y, c, a, (b + d) % self.n) for d in range(1, self.n)]
        peers += [((y + d) % self.n, c, a, b) for d in range(1, self.n)]
        peers += [((y + d) % self.n, 1 - c, a, b) for d in range(1, self.n)]
        barrier = pltpu.get_barrier_semaphore()
        for peer in peers:
            pl.semaphore_signal(barrier, inc=1, device_id=self.device(*peer), device_id_type=MESH)
        pl.semaphore_wait(barrier, len(peers))


def others_first(n):
    return [*range(1, n), 0]


def remote(src, dst, send_sem, recv_sem, device):
    return pltpu.make_async_remote_copy(
        src_ref=src, dst_ref=dst, send_sem=send_sem, recv_sem=recv_sem, device_id=device, device_id_type=MESH
    )


def density_kernel(
    rows, cols, occ, full, held, win, xsend, xrecv, acc, zsend, zrecv, shard,
    load_sem, wsend, wrecv, xs_sem, xr_sem, zs_sem, zr_sem, gu_sem, gd_sem, gi_sem, go_sem, gp_sem, gr_sem, own_sem,
):
    at = Place(rows, cols)
    n, A = at.n, at.A
    y, core, a, b = at.mine()
    own_rows, slab = shard.shape
    half = slab // 2
    depth = held.shape[0]
    sibling = at.device(y, 1 - core, a, b)
    parts = parts_of(own_rows)
    sub = own_rows // parts
    per = n * A
    steps = parts * per

    def block(k):
        j = k % per
        return k // per, (j // A + 1) % n, (j + 1) % A

    def load(k):
        s, db, dz = block(k)
        col = (a + dz) % A * n + (b + db) % n
        start = pl.multiple_of(col * own_rows + s * sub, sub)
        return pltpu.make_async_copy(occ.at[pl.ds(start, sub)], held.at[k % depth], load_sem.at[k % depth])

    for k in range(min(depth, steps)):
        load(k).start()
    at.greet()

    def part(ref, h):
        return ref.at[pl.ds(h * half, half)]

    root = (y == 0) & (core == 0)
    beside = (y == 0) & (core == 1)

    def window_sends():
        sends = []
        for d in range(1, n):
            for h in range(2):
                sends.append((h, at.device((y + d) % n, h, a, b)))
        sends += [(0, sibling), (1, sibling)]
        return [
            remote(part(occ, h), part(win, h), wsend.at[i], wrecv.at[h], device)
            for i, (h, device) in enumerate(sends)
        ]

    def window_wait(h):
        remote(part(occ, h), part(win, h), wsend.at[0], wrecv.at[h], sibling).wait_recv()

    def window_forward(h):
        return remote(part(win, h), part(win, h), wsend.at[0], wrecv.at[h], sibling)

    @pl.when(root)
    def _():
        for send in window_sends():
            send.start()
        keep = pltpu.make_async_copy(occ.at[pl.ds(0, slab)], win, own_sem.at[0])
        keep.start()
        keep.wait()

    @pl.when(beside)
    def _():
        window_wait(0)
        window_wait(1)

    for h in range(2):
        @pl.when((y > 0) & (core == h))
        def _(h=h):
            window_wait(h)
            window_forward(h).start()
            window_wait(1 - h)

    def rows_in(s):
        return pl.ds(s * sub, sub)

    def x_slot(db, dz):
        return (db - 1) * A + (a + dz) % A

    def x_copy(s, db, dz):
        slot = x_slot(db, dz)
        device = at.device(y, core, a, (b + db) % n)
        return remote(
            xsend.at[slot, rows_in(s)], xrecv.at[slot, rows_in(s)], xs_sem.at[slot, s], xr_sem.at[slot, s], device
        )

    def z_copy(s, dz):
        device = at.device(y, core, (a + dz) % A, b)
        return remote(
            zsend.at[dz - 1, rows_in(s)], zrecv.at[dz - 1, rows_in(s)],
            zs_sem.at[dz - 1, s], zr_sem.at[dz - 1, s], device,
        )

    def product(k):
        load(k).wait()
        value = lax.dot_general(
            held[k % depth], win[...], (((1,), (1,)), ((), ())), preferred_element_type=F32
        )
        return value

    def refill(k):
        @pl.when(k + depth < steps)
        def _():
            load(k + depth).start()

    def send_products(s):
        @pl.loop(s * per, s * per + per - A)
        def _(k):
            _, db, dz = block(k)
            xsend[x_slot(db, dz), rows_in(s), :] = product(k).astype(BF16)
            x_copy(s, db, dz).start()
            refill(k)

    def keep_products(s):
        @pl.loop(s * per + per - A, s * per + per)
        def _(k):
            _, _, dz = block(k)
            acc[dz, rows_in(s), :] = product(k)
            refill(k)

    def sum_b(s):
        for dz in others_first(A):
            for db in range(1, n):
                x_copy(s, db, dz).wait_recv()
            total = acc[dz, rows_in(s), :]
            for db in range(1, n):
                total = total + xrecv[x_slot(db, dz), rows_in(s), :].astype(F32)
            if dz:
                zsend[dz - 1, rows_in(s), :] = total.astype(BF16)
                z_copy(s, dz).start()
            else:
                acc[0, rows_in(s), :] = total

    outer, inner = at.sides(core)

    def rows_of(s, owner):
        return full.at[pl.ds(pl.multiple_of(owner * own_rows + s * sub, sub), sub)]

    def copy_of(src, s, owner, sems, i, device):
        return remote(src, rows_of(s, owner), sems.at[s, i], gr_sem.at[owner, s], device)

    def arrived(s, owner):
        copy_of(rows_of(s, owner), s, owner, gp_sem, 0, sibling).wait_recv()

    def shard_at(do, di, pa):
        py, pb = at.from_sides(core, (outer + do) % n, (inner + di) % n)
        return at.owner(py, core, pa, pb)

    def device_at(do, di, pa):
        py, pb = at.from_sides(core, (outer + do) % n, (inner + di) % n)
        return at.device(py, core, pa, pb)

    def to_sibling(src, s, do, di, pa):
        return copy_of(src, s, shard_at(-do, -di, pa), gp_sem, (do * n + di) * A + pa, sibling)

    def to_outer(src, s, di, pa):
        return [
            copy_of(src, s, shard_at(0, -di, pa), go_sem, ((d - 1) * n + di) * A + pa, device_at(d, 0, a))
            for d in range(1, n)
        ]

    def to_inner(src, s, pa):
        return [
            copy_of(src, s, shard_at(0, 0, pa), gi_sem, (d - 1) * A + pa, device_at(0, d, a))
            for d in range(1, n)
        ]

    def to_up(src, s, pa):
        return copy_of(src, s, shard_at(0, 0, pa), gu_sem, pa, at.device(y, core, (a + 1) % A, b))

    def to_down(src, s, pa):
        return copy_of(src, s, shard_at(0, 0, pa), gd_sem, pa, at.device(y, core, (a + A - 1) % A, b))

    mine = at.owner(y, core, a, b)

    def keep_copy(s):
        return pltpu.make_async_copy(shard.at[rows_in(s)], rows_of(s, mine), own_sem.at[s])

    def finish(s):
        total = acc[0, rows_in(s), :]
        for dz in range(1, A):
            z_copy(s, dz).wait_recv()
            total = total + zrecv[dz - 1, rows_in(s), :].astype(F32)
        shard[rows_in(s), :] = total.astype(BF16)
        own = shard.at[rows_in(s)]

        @pl.when(a < A - 1)
        def _():
            to_up(own, s, a).start()

        @pl.when(a > 0)
        def _():
            to_down(own, s, a).start()

        for copy in to_outer(own, s, 0, a) + to_inner(own, s, a):
            copy.start()
        to_sibling(own, s, 0, 0, a).start()
        keep_copy(s).start()

    def along_a(s, j):
        def pass_on(pa, further, send):
            owner = shard_at(0, 0, pa)
            arrived(s, owner)
            src = rows_of(s, owner)

            @pl.when(further)
            def _():
                send(src, s, pa).start()

            for copy in to_outer(src, s, 0, pa) + to_inner(src, s, pa):
                copy.start()
            to_sibling(src, s, 0, 0, pa).start()

        @pl.when(a - j >= 0)
        def _():
            pass_on(a - j, a < A - 1, to_up)

        @pl.when(a + j < A)
        def _():
            pass_on(a + j, a > 0, to_down)

    def along_inner(s):
        for dz in near_first:
            for di in range(1, n):
                pa = (a + dz) % A
                owner = shard_at(0, -di, pa)
                arrived(s, owner)
                for copy in to_outer(rows_of(s, owner), s, di, pa):
                    copy.start()
                to_sibling(rows_of(s, owner), s, 0, di, pa).start()

    def along_outer(s):
        for di in range(n):
            for dz in near_first:
                for do in range(1, n):
                    pa = (a + dz) % A
                    owner = shard_at(-do, -di, pa)
                    arrived(s, owner)
                    to_sibling(rows_of(s, owner), s, do, di, pa).start()

    near_first = sorted(range(A), key=lambda d: min(d, A - d))

    def stage(name, s):
        if 0 <= s < parts:
            name(s)

    def spread_a(s):
        for j in range(1, A):
            along_a(s, j)

    for s in range(parts + 5):
        stage(send_products, s)
        stage(sum_b, s - 1)
        stage(keep_products, s)
        stage(finish, s - 2)
        stage(spread_a, s - 3)
        stage(along_inner, s - 3)
        stage(along_outer, s - 4)

    for s in range(parts):
        @pl.loop(0, n * A * n)
        def _(q, s=s):
            py, pa, pb = q // (A * n), q // n % A, q % n
            arrived(s, at.owner(py, 1 - core, pa, pb))

    for s in range(parts):
        keep_copy(s).wait()

        @pl.loop(0, A)
        def _(pa, s=s):
            src = shard.at[rows_in(s)]

            @pl.when((pa <= a) & (a < A - 1))
            def _():
                to_up(src, s, pa).wait_send()

            @pl.when((pa >= a) & (a > 0))
            def _():
                to_down(src, s, pa).wait_send()

            for copy in to_inner(src, s, pa):
                copy.wait_send()
            for di in range(n):
                for copy in to_outer(src, s, di, pa):
                    copy.wait_send()
                for do in range(n):
                    to_sibling(src, s, do, di, pa).wait_send()
            for db in range(1, n):
                x_copy(s, db, (pa + A - a) % A).wait_send()

        for dz in range(1, A):
            z_copy(s, dz).wait_send()

    @pl.when(root)
    def _():
        for send in window_sends():
            send.wait_send()

    for h in range(2):
        @pl.when((y > 0) & (core == h))
        def _(h=h):
            window_forward(h).wait_send()


def parts_of(own_rows):
    return next(parts for parts in (3, 2, 1) if own_rows % (parts * 16) == 0)


def gathered_density(occ_coeffs, slab):
    rows, cols = lax.axis_size("row"), lax.axis_size("col")
    n = rows // 2
    A = cols // n
    group_rows, depth = occ_coeffs.shape
    own_rows = group_rows // cols
    owners = rows * cols
    parts = parts_of(own_rows)
    side = (n - 1) * A
    dma = pltpu.SemaphoreType.DMA
    return pl.pallas_call(
        functools.partial(density_kernel, rows, cols),
        out_shape=jax.ShapeDtypeStruct((group_rows * rows, slab), BF16),
        in_specs=[pl.BlockSpec(memory_space=pl.ANY)],
        out_specs=pl.BlockSpec(memory_space=pl.ANY),
        scratch_shapes=[
            pltpu.VMEM((HELD, own_rows // parts, depth), BF16),
            pltpu.VMEM((slab, depth), BF16),
            pltpu.VMEM(((n - 1) * A, own_rows, slab), BF16),
            pltpu.VMEM(((n - 1) * A, own_rows, slab), BF16),
            pltpu.VMEM((A, own_rows, slab), F32),
            pltpu.VMEM((A - 1, own_rows, slab), BF16),
            pltpu.VMEM((A - 1, own_rows, slab), BF16),
            pltpu.VMEM((own_rows, slab), BF16),
            dma((HELD,)),
            dma((2 * n,)),
            dma((2,)),
            dma((side, parts)),
            dma((side, parts)),
            dma((A - 1, parts)),
            dma((A - 1, parts)),
            dma((parts, A)),
            dma((parts, A)),
            dma((parts, side)),
            dma((parts, side * n)),
            dma((parts, A * n * n)),
            dma((owners, parts)),
            dma((parts,)),
        ],
        compiler_params=pltpu.CompilerParams(
            collective_id=0, has_side_effects=True, vmem_limit_bytes=VMEM_BYTES
        ),
        name="density_everywhere",
    )(occ_coeffs)


def batch_kernel(
    lists, counts, full, colloc, points, weights, charge_sites, proj, dense, fetched, term, rows, sites, fetch_sem
):
    i = pl.program_id(0)
    steps = pl.num_programs(0)
    total_points = colloc.shape[2]
    chunk = min(256, total_points)

    def fetch(step, s):
        start = pl.multiple_of(lists[step, s] * SH, SH)
        return pltpu.make_async_copy(
            full.at[pl.ds(start, SH)], fetched.at[step % 2, pl.ds(s * SH, SH)], fetch_sem.at[step % 2, s]
        )

    @pl.when(i == 0)
    def _():
        for s in range(NSIG):
            fetch(i, s).start()
        rows[...] = jnp.zeros(rows.shape, F32)
        rows[0:3, :] = charge_sites[...]
        sites[...] = rows[...].T
        blank = dense.shape[0] // 64

        @pl.loop(0, 64)
        def _(t):
            dense[pl.ds(pl.multiple_of(t * blank, blank), blank), :] = jnp.zeros((blank, dense.shape[1]), dense.dtype)

    @pl.when(i + 1 < steps)
    def _():
        for s in range(NSIG):
            fetch(i + 1, s).start()

    for s in range(NSIG):
        fetch(i, s).wait()
    count = counts[i]

    def point_chunk(j):
        cut = slice(j * chunk, (j + 1) * chunk)
        values = colloc[0, :, cut]
        field = lax.dot_general(
            fetched[i % 2], values, (((0,), (0,)), ((), ())), preferred_element_type=F32
        ).astype(BF16)
        projected = jnp.dot(proj[...], field, preferred_element_type=F32)
        live = (j * chunk + lax.broadcasted_iota(jnp.int32, (1, chunk), 1) < count).astype(F32)
        dist_sq = (points[0, 0:1, cut] - sites[:, 0:1]) ** 2
        dist_sq = dist_sq + (points[0, 1:2, cut] - sites[:, 1:2]) ** 2
        dist_sq = dist_sq + (points[0, 2:3, cut] - sites[:, 2:3]) ** 2
        kernel = lax.rsqrt(dist_sq + SMEAR_SQ)
        charges = (projected * kernel * (weights[pl.ds(i, 1), cut] * live)).astype(BF16)
        spread = lax.dot_general(
            proj[...], charges, (((0,), (0,)), ((), ())), preferred_element_type=F32
        ).astype(BF16)
        return lax.dot_general(values, spread, (((1,), (1,)), ((), ())), preferred_element_type=F32)

    term[...] = point_chunk(0)
    for j in range(1, total_points // chunk):
        @pl.when(count > j * chunk)
        def _(j=j):
            term[...] += point_chunk(j)

    for s in range(NSIG):
        start = pl.multiple_of(lists[i, s] * SH, SH)
        dense[pl.ds(start, SH), :] = term[s * SH:(s + 1) * SH, :].astype(dense.dtype)


def batch_terms(full, colloc, grid_points, grid_weights, charge_sites, charge_proj, shell_lists, point_counts):
    batches, func_rows, total_points = colloc.shape
    slab = full.shape[1]
    aux = charge_proj.shape[0]
    return pl.pallas_call(
        batch_kernel,
        out_shape=jax.ShapeDtypeStruct(full.shape, BF16),
        grid_spec=pltpu.PrefetchScalarGridSpec(
            num_scalar_prefetch=2,
            grid=(batches,),
            in_specs=[
                pl.BlockSpec(memory_space=pl.ANY),
                pl.BlockSpec((1, func_rows, total_points), lambda i, *_: (i, 0, 0)),
                pl.BlockSpec((1, 3, total_points), lambda i, *_: (i, 0, 0)),
                pl.BlockSpec((batches, total_points), lambda i, *_: (0, 0)),
                pl.BlockSpec((3, aux), lambda i, *_: (0, 0)),
                pl.BlockSpec((aux, slab), lambda i, *_: (0, 0)),
            ],
            out_specs=pl.BlockSpec(full.shape, lambda i, *_: (0, 0)),
            scratch_shapes=[
                pltpu.VMEM((2, func_rows, slab), BF16),
                pltpu.VMEM((func_rows, slab), F32),
                pltpu.VMEM((8, aux), F32),
                pltpu.VMEM((aux, 8), F32),
                pltpu.SemaphoreType.DMA((2, NSIG)),
            ],
        ),
        compiler_params=pltpu.CompilerParams(vmem_limit_bytes=VMEM_BYTES),
        name="batch_terms",
    )(
        shell_lists, point_counts, full, colloc, grid_points,
        grid_weights, charge_sites, charge_proj,
    )


def reduce_kernel(
    rows, cols, dense, out, own, r0, s1, r1, s2, r2, s3, r3,
    own_sem, s0_sem, r0_sem, s1_sem, r1_sem, s2_sem, r2_sem, s3_sem, r3_sem,
):
    at = Place(rows, cols)
    n, A = at.n, at.A
    y, core, a, b = at.mine()
    own_rows = out.shape[0]
    outer, inner = at.sides(core)
    sibling = at.device(y, 1 - core, a, b)
    order = [(do, di, dz) for do in others_first(n) for di in others_first(n) for dz in others_first(A)]

    def shard_of(side, do, di, dz):
        so, si = at.sides(side)
        py, pb = at.from_sides(side, (so + do) % n, (si + di) % n)
        pa = (a + dz) % A
        return at.owner(py, side, pa, pb), (py * A + pa) * n + pb

    parts = parts_of(own_rows)
    sub = own_rows // parts

    def rows_of(owner, s):
        return dense.at[pl.ds(pl.multiple_of(owner * own_rows + s * sub, sub), sub)]

    def rows_in(s):
        return pl.ds(s * sub, sub)

    def own_load(k, s):
        owner, slot = shard_of(core, *order[k])
        return pltpu.make_async_copy(rows_of(owner, s), own.at[slot, rows_in(s)], own_sem.at[slot, s])

    def pair_copy(k, s):
        owner, slot = shard_of(1 - core, *order[k])
        return remote(
            rows_of(owner, s), r0.at[slot, rows_in(s)], s0_sem.at[slot, s], r0_sem.at[slot, s], sibling
        )

    def pair_wait(slot, s):
        there = r0.at[slot, rows_in(s)]
        remote(there, there, s0_sem.at[slot, s], r0_sem.at[slot, s], sibling).wait_recv()

    def peer(do, di, dz):
        py, pb = at.from_sides(core, (outer + do) % n, (inner + di) % n)
        return at.device(py, core, (a + dz) % A, pb)

    def outer_slot(do, di, dz):
        return ((do - 1) * n + (inner + di) % n) * A + (a + dz) % A

    def inner_slot(di, dz):
        return (di - 1) * A + (a + dz) % A

    def slot_copy(src, dst, src_sem, dst_sem, slot, s, device):
        return remote(
            src.at[slot, rows_in(s)], dst.at[slot, rows_in(s)], src_sem.at[slot, s], dst_sem.at[slot, s], device
        )

    def outer_copy(do, di, dz, s):
        return slot_copy(s1, r1, s1_sem, r1_sem, outer_slot(do, di, dz), s, peer(do, 0, 0))

    def inner_copy(di, dz, s):
        return slot_copy(s2, r2, s2_sem, r2_sem, inner_slot(di, dz), s, peer(0, di, 0))

    def last_copy(dz, s):
        return slot_copy(s3, r3, s3_sem, r3_sem, dz - 1, s, peer(0, 0, dz))

    for s in range(parts):
        for k in range(len(order)):
            own_load(k, s).start()
    at.greet()
    for s in range(parts):
        for k in range(len(order)):
            pair_copy(k, s).start()

    def add_up(k, s):
        do, di, dz = order[k]
        _, slot = shard_of(core, do, di, dz)
        rows = rows_in(s)
        own_load(k, s).wait()
        pair_wait(slot, s)
        total = own[slot, rows, :].astype(F32) + r0[slot, rows, :].astype(F32)
        if do:
            s1[outer_slot(do, di, dz), rows, :] = total.astype(BF16)
            outer_copy(do, di, dz, s).start()
            return
        for d in range(1, n):
            outer_copy(d, di, dz, s).wait_recv()
            total = total + r1[outer_slot(d, di, dz), rows, :].astype(F32)
        if di:
            s2[inner_slot(di, dz), rows, :] = total.astype(BF16)
            inner_copy(di, dz, s).start()
            return
        for d in range(1, n):
            inner_copy(d, dz, s).wait_recv()
            total = total + r2[inner_slot(d, dz), rows, :].astype(F32)
        if dz:
            s3[dz - 1, rows, :] = total.astype(BF16)
            last_copy(dz, s).start()
            return
        for d in range(1, A):
            last_copy(d, s).wait_recv()
            total = total + r3[d - 1, rows, :].astype(F32)
        out[rows, :] = total

    def level(place):
        do, di, dz = place
        return 0 if do else 1 if di else 2 if dz else 3

    for step in range(parts + 3):
        for stage in range(4):
            s = step - stage
            if 0 <= s < parts:
                for k, place in enumerate(order):
                    if level(place) == stage:
                        add_up(k, s)

    for s in range(parts):
        for k, (do, di, dz) in enumerate(order):
            pair_copy(k, s).wait_send()
            if do:
                outer_copy(do, di, dz, s).wait_send()
            elif di:
                inner_copy(di, dz, s).wait_send()
            elif dz:
                last_copy(dz, s).wait_send()


def reduced_to_owners(dense):
    rows, cols = lax.axis_size("row"), lax.axis_size("col")
    n = rows // 2
    A = cols // n
    slab = dense.shape[1]
    own_rows = dense.shape[0] // (rows * cols)
    half = rows * cols // 2
    parts = parts_of(own_rows)
    dma = pltpu.SemaphoreType.DMA

    def buffer(count):
        return pltpu.VMEM((count, own_rows, slab), BF16)

    outer, inner = (n - 1) * n * A, (n - 1) * A
    return pl.pallas_call(
        functools.partial(reduce_kernel, rows, cols),
        out_shape=jax.ShapeDtypeStruct((own_rows, slab), F32),
        in_specs=[pl.BlockSpec(memory_space=pl.ANY)],
        out_specs=pl.BlockSpec(memory_space=pltpu.VMEM),
        scratch_shapes=[
            buffer(half), buffer(half),
            buffer(outer), buffer(outer),
            buffer(inner), buffer(inner),
            buffer(A - 1), buffer(A - 1),
            dma((half, parts)), dma((half, parts)), dma((half, parts)),
            dma((outer, parts)), dma((outer, parts)),
            dma((inner, parts)), dma((inner, parts)),
            dma((A - 1, parts)), dma((A - 1, parts)),
        ],
        compiler_params=pltpu.CompilerParams(
            collective_id=1, has_side_effects=True, vmem_limit_bytes=VMEM_BYTES
        ),
        name="reduce_to_owners",
    )(dense)


def on_device(
    occ_coeffs, colloc, grid_points, grid_weights, charge_sites, charge_proj, shell_lists, point_counts
):
    full = gathered_density(occ_coeffs, charge_proj.shape[1])
    dense = batch_terms(
        full, colloc, grid_points, grid_weights, charge_sites, charge_proj, shell_lists, point_counts
    )
    return reduced_to_owners(dense)


def solution(mesh):
    placed = (
        P("row", "col"),
        P(("row", "col"), None, None),
        P(("row", "col"), None, None),
        P(("row", "col"), None),
        P(),
        P(),
        P(("row", "col"), None),
        P(("row", "col")),
    )
    return jax.shard_map(
        on_device, mesh=mesh, in_specs=placed, out_specs=P(("row", "col"), None), check_vma=False
    )
```

```python
import functools

import jax
import jax.numpy as jnp
from jax import lax
from jax.experimental import pallas as pl
from jax.experimental.pallas import tpu as pltpu
from jax.sharding import PartitionSpec as P

SH = 64
NSIG = 16
SMEAR_SQ = 0.25
MESH = pl.DeviceIdType.MESH
F32 = jnp.float32
BF16 = jnp.bfloat16
VMEM_BYTES = 58 * 1024 * 1024
HELD = 16


class Place:
    def __init__(self, rows, cols):
        self.n = rows // 2
        self.A = cols // self.n
        self.cols = cols
        row, col = lax.axis_index("row"), lax.axis_index("col")
        self.y, self.core = row // 2, row % 2
        self.a, self.b = col // self.n, col % self.n

    def device(self, y, core, a, b):
        return (y * 2 + core, a * self.n + b)

    def mine(self):
        return self.y, self.core, self.a, self.b

    def sides(self, core):
        return self.y * (1 - core) + self.b * core, self.b * (1 - core) + self.y * core

    def from_sides(self, core, outer, inner):
        return outer * (1 - core) + inner * core, inner * (1 - core) + outer * core

    def owner(self, y, core, a, b):
        return (y * 2 + core) * self.cols + a * self.n + b

    def greet(self):
        y, c, a, b = self.mine()
        peers = [(y, 1 - c, a, b)]
        peers += [(y, c, (a + d) % self.A, b) for d in range(1, self.A)]
        peers += [(y, c, a, (b + d) % self.n) for d in range(1, self.n)]
        peers += [((y + d) % self.n, c, a, b) for d in range(1, self.n)]
        peers += [((y + d) % self.n, 1 - c, a, b) for d in range(1, self.n)]
        barrier = pltpu.get_barrier_semaphore()
        for peer in peers:
            pl.semaphore_signal(barrier, inc=1, device_id=self.device(*peer), device_id_type=MESH)
        pl.semaphore_wait(barrier, len(peers))


def others_first(n):
    return [*range(1, n), 0]


def remote(src, dst, send_sem, recv_sem, device):
    return pltpu.make_async_remote_copy(
        src_ref=src, dst_ref=dst, send_sem=send_sem, recv_sem=recv_sem, device_id=device, device_id_type=MESH
    )


def density_kernel(
    rows, cols, occ, full, held, win, xsend, xrecv, acc, zsend, zrecv, shard,
    load_sem, wsend, wrecv, xs_sem, xr_sem, zs_sem, zr_sem, gu_sem, gd_sem, gi_sem, go_sem, gp_sem, gr_sem, own_sem,
):
    at = Place(rows, cols)
    n, A = at.n, at.A
    y, core, a, b = at.mine()
    own_rows, slab = shard.shape
    half = slab // 2
    depth = held.shape[0]
    sibling = at.device(y, 1 - core, a, b)
    parts = parts_of(own_rows)
    sub = own_rows // parts
    per = n * A
    steps = parts * per

    def block(k):
        j = k % per
        return k // per, (j // A + 1) % n, (j + 1) % A

    def load(k):
        s, db, dz = block(k)
        col = (a + dz) % A * n + (b + db) % n
        start = pl.multiple_of(col * own_rows + s * sub, sub)
        return pltpu.make_async_copy(occ.at[pl.ds(start, sub)], held.at[k % depth], load_sem.at[k % depth])

    for k in range(min(depth, steps)):
        load(k).start()
    at.greet()

    def part(ref, h):
        return ref.at[pl.ds(h * half, half)]

    root = (y == 0) & (core == 0)
    beside = (y == 0) & (core == 1)

    def window_sends():
        sends = []
        for d in range(1, n):
            for h in range(2):
                sends.append((h, at.device((y + d) % n, h, a, b)))
        sends += [(0, sibling), (1, sibling)]
        return [
            remote(part(occ, h), part(win, h), wsend.at[i], wrecv.at[h], device)
            for i, (h, device) in enumerate(sends)
        ]

    def window_wait(h):
        remote(part(occ, h), part(win, h), wsend.at[0], wrecv.at[h], sibling).wait_recv()

    def window_forward(h):
        return remote(part(win, h), part(win, h), wsend.at[0], wrecv.at[h], sibling)

    @pl.when(root)
    def _():
        for send in window_sends():
            send.start()
        keep = pltpu.make_async_copy(occ.at[pl.ds(0, slab)], win, own_sem.at[0])
        keep.start()
        keep.wait()

    @pl.when(beside)
    def _():
        window_wait(0)
        window_wait(1)

    for h in range(2):
        @pl.when((y > 0) & (core == h))
        def _(h=h):
            window_wait(h)
            window_forward(h).start()
            window_wait(1 - h)

    def rows_in(s):
        return pl.ds(s * sub, sub)

    def x_slot(db, dz):
        return (db - 1) * A + (a + dz) % A

    def x_copy(s, db, dz):
        slot = x_slot(db, dz)
        device = at.device(y, core, a, (b + db) % n)
        return remote(
            xsend.at[slot, rows_in(s)], xrecv.at[slot, rows_in(s)], xs_sem.at[slot, s], xr_sem.at[slot, s], device
        )

    def z_copy(s, dz):
        device = at.device(y, core, (a + dz) % A, b)
        return remote(
            zsend.at[dz - 1, rows_in(s)], zrecv.at[dz - 1, rows_in(s)],
            zs_sem.at[dz - 1, s], zr_sem.at[dz - 1, s], device,
        )

    def product(k):
        load(k).wait()
        value = lax.dot_general(
            held[k % depth], win[...], (((1,), (1,)), ((), ())), preferred_element_type=F32
        )
        return value

    def refill(k):
        @pl.when(k + depth < steps)
        def _():
            load(k + depth).start()

    def send_products(s):
        @pl.loop(s * per, s * per + per - A)
        def _(k):
            _, db, dz = block(k)
            xsend[x_slot(db, dz), rows_in(s), :] = product(k).astype(BF16)
            x_copy(s, db, dz).start()
            refill(k)

    def keep_products(s):
        @pl.loop(s * per + per - A, s * per + per)
        def _(k):
            _, _, dz = block(k)
            acc[dz, rows_in(s), :] = product(k)
            refill(k)

    def sum_b(s):
        for dz in others_first(A):
            for db in range(1, n):
                x_copy(s, db, dz).wait_recv()
            total = acc[dz, rows_in(s), :]
            for db in range(1, n):
                total = total + xrecv[x_slot(db, dz), rows_in(s), :].astype(F32)
            if dz:
                zsend[dz - 1, rows_in(s), :] = total.astype(BF16)
                z_copy(s, dz).start()
            else:
                acc[0, rows_in(s), :] = total

    outer, inner = at.sides(core)

    def rows_of(s, owner):
        return full.at[pl.ds(pl.multiple_of(owner * own_rows + s * sub, sub), sub)]

    def copy_of(src, s, owner, sems, i, device):
        return remote(src, rows_of(s, owner), sems.at[s, i], gr_sem.at[owner, s], device)

    def arrived(s, owner):
        copy_of(rows_of(s, owner), s, owner, gp_sem, 0, sibling).wait_recv()

    def shard_at(do, di, pa):
        py, pb = at.from_sides(core, (outer + do) % n, (inner + di) % n)
        return at.owner(py, core, pa, pb)

    def device_at(do, di, pa):
        py, pb = at.from_sides(core, (outer + do) % n, (inner + di) % n)
        return at.device(py, core, pa, pb)

    def to_sibling(src, s, do, di, pa):
        return copy_of(src, s, shard_at(-do, -di, pa), gp_sem, (do * n + di) * A + pa, sibling)

    def to_outer(src, s, di, pa):
        return [
            copy_of(src, s, shard_at(0, -di, pa), go_sem, ((d - 1) * n + di) * A + pa, device_at(d, 0, a))
            for d in range(1, n)
        ]

    def to_inner(src, s, pa):
        return [
            copy_of(src, s, shard_at(0, 0, pa), gi_sem, (d - 1) * A + pa, device_at(0, d, a))
            for d in range(1, n)
        ]

    def to_up(src, s, pa):
        return copy_of(src, s, shard_at(0, 0, pa), gu_sem, pa, at.device(y, core, (a + 1) % A, b))

    def to_down(src, s, pa):
        return copy_of(src, s, shard_at(0, 0, pa), gd_sem, pa, at.device(y, core, (a + A - 1) % A, b))

    mine = at.owner(y, core, a, b)

    def keep_copy(s):
        return pltpu.make_async_copy(shard.at[rows_in(s)], rows_of(s, mine), own_sem.at[s])

    def finish(s):
        total = acc[0, rows_in(s), :]
        for dz in range(1, A):
            z_copy(s, dz).wait_recv()
            total = total + zrecv[dz - 1, rows_in(s), :].astype(F32)
        shard[rows_in(s), :] = total.astype(BF16)
        own = shard.at[rows_in(s)]

        @pl.when(a < A - 1)
        def _():
            to_up(own, s, a).start()

        @pl.when(a > 0)
        def _():
            to_down(own, s, a).start()

        for copy in to_outer(own, s, 0, a) + to_inner(own, s, a):
            copy.start()
        to_sibling(own, s, 0, 0, a).start()
        keep_copy(s).start()

    def along_a(s, j):
        def pass_on(pa, further, send):
            owner = shard_at(0, 0, pa)
            arrived(s, owner)
            src = rows_of(s, owner)

            @pl.when(further)
            def _():
                send(src, s, pa).start()

            for copy in to_outer(src, s, 0, pa) + to_inner(src, s, pa):
                copy.start()
            to_sibling(src, s, 0, 0, pa).start()

        @pl.when(a - j >= 0)
        def _():
            pass_on(a - j, a < A - 1, to_up)

        @pl.when(a + j < A)
        def _():
            pass_on(a + j, a > 0, to_down)

    def along_inner(s):
        for dz in near_first:
            for di in range(1, n):
                pa = (a + dz) % A
                owner = shard_at(0, -di, pa)
                arrived(s, owner)
                for copy in to_outer(rows_of(s, owner), s, di, pa):
                    copy.start()
                to_sibling(rows_of(s, owner), s, 0, di, pa).start()

    def along_outer(s):
        for di in range(n):
            for dz in near_first:
                for do in range(1, n):
                    pa = (a + dz) % A
                    owner = shard_at(-do, -di, pa)
                    arrived(s, owner)
                    to_sibling(rows_of(s, owner), s, do, di, pa).start()

    near_first = sorted(range(A), key=lambda d: min(d, A - d))

    def stage(name, s):
        if 0 <= s < parts:
            name(s)

    def spread_a(s):
        for j in range(1, A):
            along_a(s, j)

    for s in range(parts + 5):
        stage(send_products, s)
        stage(sum_b, s - 1)
        stage(keep_products, s)
        stage(finish, s - 2)
        stage(spread_a, s - 3)
        stage(along_inner, s - 3)
        stage(along_outer, s - 4)

    for s in range(parts):
        @pl.loop(0, n * A * n)
        def _(q, s=s):
            py, pa, pb = q // (A * n), q // n % A, q % n
            arrived(s, at.owner(py, 1 - core, pa, pb))

    for s in range(parts):
        keep_copy(s).wait()

        @pl.loop(0, A)
        def _(pa, s=s):
            src = shard.at[rows_in(s)]

            @pl.when((pa <= a) & (a < A - 1))
            def _():
                to_up(src, s, pa).wait_send()

            @pl.when((pa >= a) & (a > 0))
            def _():
                to_down(src, s, pa).wait_send()

            for copy in to_inner(src, s, pa):
                copy.wait_send()
            for di in range(n):
                for copy in to_outer(src, s, di, pa):
                    copy.wait_send()
                for do in range(n):
                    to_sibling(src, s, do, di, pa).wait_send()
            for db in range(1, n):
                x_copy(s, db, (pa + A - a) % A).wait_send()

        for dz in range(1, A):
            z_copy(s, dz).wait_send()

    @pl.when(root)
    def _():
        for send in window_sends():
            send.wait_send()

    for h in range(2):
        @pl.when((y > 0) & (core == h))
        def _(h=h):
            window_forward(h).wait_send()


def parts_of(own_rows):
    return next(parts for parts in (4, 3, 2, 1) if own_rows % (parts * 16) == 0)


def gathered_density(occ_coeffs, slab):
    rows, cols = lax.axis_size("row"), lax.axis_size("col")
    n = rows // 2
    A = cols // n
    group_rows, depth = occ_coeffs.shape
    own_rows = group_rows // cols
    owners = rows * cols
    parts = parts_of(own_rows)
    side = (n - 1) * A
    dma = pltpu.SemaphoreType.DMA
    return pl.pallas_call(
        functools.partial(density_kernel, rows, cols),
        out_shape=jax.ShapeDtypeStruct((group_rows * rows, slab), BF16),
        in_specs=[pl.BlockSpec(memory_space=pl.ANY)],
        out_specs=pl.BlockSpec(memory_space=pl.ANY),
        scratch_shapes=[
            pltpu.VMEM((HELD, own_rows // parts, depth), BF16),
            pltpu.VMEM((slab, depth), BF16),
            pltpu.VMEM(((n - 1) * A, own_rows, slab), BF16),
            pltpu.VMEM(((n - 1) * A, own_rows, slab), BF16),
            pltpu.VMEM((A, own_rows, slab), F32),
            pltpu.VMEM((A - 1, own_rows, slab), BF16),
            pltpu.VMEM((A - 1, own_rows, slab), BF16),
            pltpu.VMEM((own_rows, slab), BF16),
            dma((HELD,)),
            dma((2 * n,)),
            dma((2,)),
            dma((side, parts)),
            dma((side, parts)),
            dma((A - 1, parts)),
            dma((A - 1, parts)),
            dma((parts, A)),
            dma((parts, A)),
            dma((parts, side)),
            dma((parts, side * n)),
            dma((parts, A * n * n)),
            dma((owners, parts)),
            dma((parts,)),
        ],
        compiler_params=pltpu.CompilerParams(
            collective_id=0, has_side_effects=True, vmem_limit_bytes=VMEM_BYTES
        ),
        name="density_everywhere",
    )(occ_coeffs)


def batch_kernel(
    lists, counts, full, colloc, points, weights, charge_sites, proj, dense, fetched, term, rows, sites, fetch_sem
):
    i = pl.program_id(0)
    steps = pl.num_programs(0)
    total_points = colloc.shape[2]
    chunk = min(256, total_points)

    def fetch(step, s):
        start = pl.multiple_of(lists[step, s] * SH, SH)
        return pltpu.make_async_copy(
            full.at[pl.ds(start, SH)], fetched.at[step % 2, pl.ds(s * SH, SH)], fetch_sem.at[step % 2, s]
        )

    @pl.when(i == 0)
    def _():
        for s in range(NSIG):
            fetch(i, s).start()
        rows[...] = jnp.zeros(rows.shape, F32)
        rows[0:3, :] = charge_sites[...]
        sites[...] = rows[...].T
        blank = dense.shape[0] // 64

        @pl.loop(0, 64)
        def _(t):
            dense[pl.ds(pl.multiple_of(t * blank, blank), blank), :] = jnp.zeros((blank, dense.shape[1]), dense.dtype)

    @pl.when(i + 1 < steps)
    def _():
        for s in range(NSIG):
            fetch(i + 1, s).start()

    for s in range(NSIG):
        fetch(i, s).wait()
    count = counts[i]

    def point_chunk(j):
        cut = slice(j * chunk, (j + 1) * chunk)
        values = colloc[0, :, cut]
        field = lax.dot_general(
            fetched[i % 2], values, (((0,), (0,)), ((), ())), preferred_element_type=F32
        ).astype(BF16)
        projected = jnp.dot(proj[...], field, preferred_element_type=F32)
        live = (j * chunk + lax.broadcasted_iota(jnp.int32, (1, chunk), 1) < count).astype(F32)
        dist_sq = (points[0, 0:1, cut] - sites[:, 0:1]) ** 2
        dist_sq = dist_sq + (points[0, 1:2, cut] - sites[:, 1:2]) ** 2
        dist_sq = dist_sq + (points[0, 2:3, cut] - sites[:, 2:3]) ** 2
        kernel = lax.rsqrt(dist_sq + SMEAR_SQ)
        charges = (projected * kernel * (weights[pl.ds(i, 1), cut] * live)).astype(BF16)
        spread = lax.dot_general(
            proj[...], charges, (((0,), (0,)), ((), ())), preferred_element_type=F32
        ).astype(BF16)
        return lax.dot_general(values, spread, (((1,), (1,)), ((), ())), preferred_element_type=F32)

    term[...] = point_chunk(0)
    for j in range(1, total_points // chunk):
        @pl.when(count > j * chunk)
        def _(j=j):
            term[...] += point_chunk(j)

    for s in range(NSIG):
        start = pl.multiple_of(lists[i, s] * SH, SH)
        dense[pl.ds(start, SH), :] = term[s * SH:(s + 1) * SH, :].astype(dense.dtype)


def batch_terms(full, colloc, grid_points, grid_weights, charge_sites, charge_proj, shell_lists, point_counts):
    batches, func_rows, total_points = colloc.shape
    slab = full.shape[1]
    aux = charge_proj.shape[0]
    return pl.pallas_call(
        batch_kernel,
        out_shape=jax.ShapeDtypeStruct(full.shape, BF16),
        grid_spec=pltpu.PrefetchScalarGridSpec(
            num_scalar_prefetch=2,
            grid=(batches,),
            in_specs=[
                pl.BlockSpec(memory_space=pl.ANY),
                pl.BlockSpec((1, func_rows, total_points), lambda i, *_: (i, 0, 0)),
                pl.BlockSpec((1, 3, total_points), lambda i, *_: (i, 0, 0)),
                pl.BlockSpec((batches, total_points), lambda i, *_: (0, 0)),
                pl.BlockSpec((3, aux), lambda i, *_: (0, 0)),
                pl.BlockSpec((aux, slab), lambda i, *_: (0, 0)),
            ],
            out_specs=pl.BlockSpec(full.shape, lambda i, *_: (0, 0)),
            scratch_shapes=[
                pltpu.VMEM((2, func_rows, slab), BF16),
                pltpu.VMEM((func_rows, slab), F32),
                pltpu.VMEM((8, aux), F32),
                pltpu.VMEM((aux, 8), F32),
                pltpu.SemaphoreType.DMA((2, NSIG)),
            ],
        ),
        compiler_params=pltpu.CompilerParams(vmem_limit_bytes=VMEM_BYTES),
        name="batch_terms",
    )(
        shell_lists, point_counts, full, colloc, grid_points,
        grid_weights, charge_sites, charge_proj,
    )


def reduce_kernel(
    rows, cols, dense, out, own, r0, s1, r1, s2, r2, s3, r3,
    own_sem, s0_sem, r0_sem, s1_sem, r1_sem, s2_sem, r2_sem, s3_sem, r3_sem,
):
    at = Place(rows, cols)
    n, A = at.n, at.A
    y, core, a, b = at.mine()
    own_rows = out.shape[0]
    outer, inner = at.sides(core)
    sibling = at.device(y, 1 - core, a, b)
    order = [(do, di, dz) for do in others_first(n) for di in others_first(n) for dz in others_first(A)]

    def shard_of(side, do, di, dz):
        so, si = at.sides(side)
        py, pb = at.from_sides(side, (so + do) % n, (si + di) % n)
        pa = (a + dz) % A
        return at.owner(py, side, pa, pb), (py * A + pa) * n + pb

    parts = parts_of(own_rows)
    sub = own_rows // parts

    def rows_of(owner, s):
        return dense.at[pl.ds(pl.multiple_of(owner * own_rows + s * sub, sub), sub)]

    def rows_in(s):
        return pl.ds(s * sub, sub)

    def own_load(k, s):
        owner, slot = shard_of(core, *order[k])
        return pltpu.make_async_copy(rows_of(owner, s), own.at[slot, rows_in(s)], own_sem.at[slot, s])

    def pair_copy(k, s):
        owner, slot = shard_of(1 - core, *order[k])
        return remote(
            rows_of(owner, s), r0.at[slot, rows_in(s)], s0_sem.at[slot, s], r0_sem.at[slot, s], sibling
        )

    def pair_wait(slot, s):
        there = r0.at[slot, rows_in(s)]
        remote(there, there, s0_sem.at[slot, s], r0_sem.at[slot, s], sibling).wait_recv()

    def peer(do, di, dz):
        py, pb = at.from_sides(core, (outer + do) % n, (inner + di) % n)
        return at.device(py, core, (a + dz) % A, pb)

    def outer_slot(do, di, dz):
        return ((do - 1) * n + (inner + di) % n) * A + (a + dz) % A

    def inner_slot(di, dz):
        return (di - 1) * A + (a + dz) % A

    def slot_copy(src, dst, src_sem, dst_sem, slot, s, device):
        return remote(
            src.at[slot, rows_in(s)], dst.at[slot, rows_in(s)], src_sem.at[slot, s], dst_sem.at[slot, s], device
        )

    def outer_copy(do, di, dz, s):
        return slot_copy(s1, r1, s1_sem, r1_sem, outer_slot(do, di, dz), s, peer(do, 0, 0))

    def inner_copy(di, dz, s):
        return slot_copy(s2, r2, s2_sem, r2_sem, inner_slot(di, dz), s, peer(0, di, 0))

    def last_copy(dz, s):
        return slot_copy(s3, r3, s3_sem, r3_sem, dz - 1, s, peer(0, 0, dz))

    for s in range(parts):
        for k in range(len(order)):
            own_load(k, s).start()
    at.greet()
    for s in range(parts):
        for k in range(len(order)):
            pair_copy(k, s).start()

    def add_up(k, s):
        do, di, dz = order[k]
        _, slot = shard_of(core, do, di, dz)
        rows = rows_in(s)
        own_load(k, s).wait()
        pair_wait(slot, s)
        total = own[slot, rows, :].astype(F32) + r0[slot, rows, :].astype(F32)
        if do:
            s1[outer_slot(do, di, dz), rows, :] = total.astype(BF16)
            outer_copy(do, di, dz, s).start()
            return
        for d in range(1, n):
            outer_copy(d, di, dz, s).wait_recv()
            total = total + r1[outer_slot(d, di, dz), rows, :].astype(F32)
        if di:
            s2[inner_slot(di, dz), rows, :] = total.astype(BF16)
            inner_copy(di, dz, s).start()
            return
        for d in range(1, n):
            inner_copy(d, dz, s).wait_recv()
            total = total + r2[inner_slot(d, dz), rows, :].astype(F32)
        if dz:
            s3[dz - 1, rows, :] = total.astype(BF16)
            last_copy(dz, s).start()
            return
        for d in range(1, A):
            last_copy(d, s).wait_recv()
            total = total + r3[d - 1, rows, :].astype(F32)
        out[rows, :] = total

    def level(place):
        do, di, dz = place
        return 0 if do else 1 if di else 2 if dz else 3

    for step in range(parts + 3):
        for stage in range(4):
            s = step - stage
            if 0 <= s < parts:
                for k, place in enumerate(order):
                    if level(place) == stage:
                        add_up(k, s)

    for s in range(parts):
        for k, (do, di, dz) in enumerate(order):
            pair_copy(k, s).wait_send()
            if do:
                outer_copy(do, di, dz, s).wait_send()
            elif di:
                inner_copy(di, dz, s).wait_send()
            elif dz:
                last_copy(dz, s).wait_send()


def reduced_to_owners(dense):
    rows, cols = lax.axis_size("row"), lax.axis_size("col")
    n = rows // 2
    A = cols // n
    slab = dense.shape[1]
    own_rows = dense.shape[0] // (rows * cols)
    half = rows * cols // 2
    parts = parts_of(own_rows)
    dma = pltpu.SemaphoreType.DMA

    def buffer(count):
        return pltpu.VMEM((count, own_rows, slab), BF16)

    outer, inner = (n - 1) * n * A, (n - 1) * A
    return pl.pallas_call(
        functools.partial(reduce_kernel, rows, cols),
        out_shape=jax.ShapeDtypeStruct((own_rows, slab), F32),
        in_specs=[pl.BlockSpec(memory_space=pl.ANY)],
        out_specs=pl.BlockSpec(memory_space=pltpu.VMEM),
        scratch_shapes=[
            buffer(half), buffer(half),
            buffer(outer), buffer(outer),
            buffer(inner), buffer(inner),
            buffer(A - 1), buffer(A - 1),
            dma((half, parts)), dma((half, parts)), dma((half, parts)),
            dma((outer, parts)), dma((outer, parts)),
            dma((inner, parts)), dma((inner, parts)),
            dma((A - 1, parts)), dma((A - 1, parts)),
        ],
        compiler_params=pltpu.CompilerParams(
            collective_id=1, has_side_effects=True, vmem_limit_bytes=VMEM_BYTES
        ),
        name="reduce_to_owners",
    )(dense)


def on_device(
    occ_coeffs, colloc, grid_points, grid_weights, charge_sites, charge_proj, shell_lists, point_counts
):
    full = gathered_density(occ_coeffs, charge_proj.shape[1])
    dense = batch_terms(
        full, colloc, grid_points, grid_weights, charge_sites, charge_proj, shell_lists, point_counts
    )
    return reduced_to_owners(dense)


def solution(mesh):
    placed = (
        P("row", "col"),
        P(("row", "col"), None, None),
        P(("row", "col"), None, None),
        P(("row", "col"), None),
        P(),
        P(),
        P(("row", "col"), None),
        P(("row", "col")),
    )
    return jax.shard_map(
        on_device, mesh=mesh, in_specs=placed, out_specs=P(("row", "col"), None), check_vma=False
    )
```
